32 devices in a mesh: dom: 4 (over z), hid: 4 (over x, core), wt: 2 (over y).
Axes of the slice: x: 2, y: 2, z: 4, core: 2. Of those that a mesh axis runs over, the one named last changes fastest.
Arguments:
- store_feat: bfloat16 [16384, 256], P('dom'), may hold values from -6 to 6
- want_in: int32 [4, 4, 128], P('dom'), may hold values from 0 to 4095
- nbr_in: int32 [32768, 10], P('dom'), may hold values from 0 to 511
- self_in: int32 [32768], P('dom'), may hold values from 0 to 511
- count_in: int32 [32768], P('dom'), may hold values from 1 to 10
- weight_one: bfloat16 [512, 1024], P('wt', 'hid'), may hold values from -0.375 to 0.375
- want_hid: int32 [4, 4, 128], P('dom'), may hold values from 0 to 8191
- nbr_hid: int32 [8192, 15], P('dom'), may hold values from 0 to 511
- self_hid: int32 [8192], P('dom'), may hold values from 0 to 511
- count_hid: int32 [8192], P('dom'), may hold values from 1 to 15
- weight_two: bfloat16 [2048, 1024], P('wt', 'hid'), may hold values from -0.1875 to 0.1875
Outputs:
- seed_embed: bfloat16 [8192, 1024], P('dom', 'hid')
The draws below stay inside these ranges and needn't reach their ends.
Inputs may be any that keep to these rules, and one draw needn't show every extreme that they name: `count_in`: slots at or past a node's count hold arbitrary positions and are ignored. `count_hid`: slots at or past a seed's count hold arbitrary positions and are ignored.
All inputs are finite; a program needn't handle non-finite values.
Results may differ from the reference program's by a relative error of at most 0.0052.
Values may be sent and summed in bfloat16 or wider, within the bound.
A program may use at most 128 MiB of HBM per device.

```python
import math
import jax
import jax.numpy as jnp
import numpy as np
from jax import lax

F = 256
H = 1024
FAN1 = 10
FAN2 = 15
S_DEV = 4096
R0 = 128
T1 = 8192
R1 = 128
T2 = 2048
NODES = 16384
N_DOM = 4


def touch_ends(result, rng, least, top_value):
    place = [jax.random.randint(jax.random.fold_in(rng, axis), (), 0, length) for axis, length in enumerate(result.shape)]
    main_axis = result.shape.index(max(result.shape))
    next_to = place[:main_axis] + [(place[main_axis] + 1) % result.shape[main_axis]] + place[main_axis + 1:]
    return result.at[tuple(place)].set(least).at[tuple(next_to)].set(top_value)


def block_scale(rng, dims, split, smallest, high):
    def one(position, parts):
        heights = jax.random.uniform(jax.random.fold_in(jax.random.fold_in(rng, 6), position), (parts,), jnp.float32, smallest / len(split), high / len(split))
        return jnp.repeat(jnp.exp(heights), dims[position] // parts).reshape((-1,) + (1,) * (len(dims) - position - 1))

    factor_of = one(*split[0])
    for cut in split[1:]:
        factor_of = factor_of * one(*cut)
    return factor_of


def rank_table(count, skew):
    loads = [(1 << 20) // math.isqrt(standing ** skew) + 1 for standing in range(1, count + 1)]
    scale = 1 + sum(loads) // (1 << 30)
    return np.cumsum(np.array([max(1, weight // scale) for weight in loads]))


def ranked(stream_key, shape, count, lean):
    listing = rank_table(count, lean)
    lot = jax.random.randint(jax.random.fold_in(stream_key, 1), shape, 0, int(listing[count - 1]))
    standing = jnp.searchsorted(jnp.asarray(listing, jnp.int32), lot, side="right")
    return jax.random.permutation(jax.random.fold_in(stream_key, 2), count)[standing].astype(jnp.int32)


def noise(key, extent, scale, limit, split=(), held_as=jnp.bfloat16):
    factor_of = block_scale(key, extent, split, -0.22, 0.18) if split else 1.0
    drawn = jax.random.normal(key, extent, jnp.float32) * scale * factor_of
    return jnp.minimum(jnp.maximum(drawn, -limit), limit).astype(held_as)


def setup_inputs(seed: int = 0) -> dict:
    keys = jax.random.split(jax.random.key(seed), 12)
    return {
        "store_feat": noise(keys[0], (NODES, F), 1.0, 6.0, ((0, 4),)),
        "want_in": touch_ends(jax.random.randint(keys[1], (N_DOM, N_DOM, R0), 0, S_DEV), jax.random.fold_in(keys[1], 1), 0, S_DEV - 1).astype(jnp.int32),
        "nbr_in": touch_ends(ranked(keys[2], (N_DOM * T1, FAN1), N_DOM * R0, 2), jax.random.fold_in(keys[2], 3), 0, (N_DOM * R0) - 1).astype(jnp.int32),
        "self_in": touch_ends(jax.random.randint(keys[3], (N_DOM * T1,), 0, N_DOM * R0), jax.random.fold_in(keys[3], 1), 0, (N_DOM * R0) - 1).astype(jnp.int32),
        "count_in": touch_ends(jax.random.randint(keys[4], (N_DOM * T1,), 1, FAN1 + 1), jax.random.fold_in(keys[4], 1), 1, FAN1).astype(jnp.int32),
        "weight_one": noise(keys[5], (2 * F, H), F ** -0.5, 0.375, ((0, 2), (1, 4))),
        "want_hid": touch_ends(jax.random.randint(keys[6], (N_DOM, N_DOM, R1), 0, T1), jax.random.fold_in(keys[6], 1), 0, T1 - 1).astype(jnp.int32),
        "nbr_hid": touch_ends(ranked(keys[7], (N_DOM * T2, FAN2), N_DOM * R1, 2), jax.random.fold_in(keys[7], 3), 0, (N_DOM * R1) - 1).astype(jnp.int32),
        "self_hid": touch_ends(jax.random.randint(keys[8], (N_DOM * T2,), 0, N_DOM * R1), jax.random.fold_in(keys[8], 1), 0, (N_DOM * R1) - 1).astype(jnp.int32),
        "count_hid": touch_ends(jax.random.randint(keys[9], (N_DOM * T2,), 1, FAN2 + 1), jax.random.fold_in(keys[9], 1), 1, FAN2).astype(jnp.int32),
        "weight_two": noise(keys[10], (2 * H, H), H ** -0.5, 0.1875, ((0, 2), (1, 4))),
    }


def average(lookup, neighbours, counts):
    gathered = jnp.take(lookup, neighbours, axis=0).astype(jnp.float32)
    valid_mask = (lax.broadcasted_iota(jnp.int32, neighbours.shape, 1) < counts[:, None]).astype(jnp.float32)
    summed = jnp.einsum("tk,tkf->tf", valid_mask, gathered)
    return (summed / counts[:, None].astype(jnp.float32)).astype(jnp.bfloat16)


def reference(store_feat, want_in, nbr_in, self_in, count_in, weight_one, want_hid, nbr_hid, self_hid, count_hid, weight_two):
    storage = store_feat.reshape(N_DOM, S_DEV, F)
    owners = jnp.arange(N_DOM, dtype=jnp.int32)[:, None]

    def layer_one(inputs):
        wanted, neighbours, own_pos, counts = inputs
        lookup = storage[owners, wanted].reshape(N_DOM * R0, F)
        own_rows = jnp.take(lookup, own_pos, axis=0)
        mean_rows = average(lookup, neighbours, counts)
        joined = jnp.concatenate([own_rows, mean_rows], 1)
        return jax.nn.relu(jnp.dot(joined, weight_one, preferred_element_type=jnp.float32)).astype(jnp.bfloat16)

    hidden = lax.map(layer_one, (jnp.swapaxes(want_in, 0, 1), nbr_in.reshape(N_DOM, T1, FAN1), self_in.reshape(N_DOM, T1), count_in.reshape(N_DOM, T1)))

    def layer_two(inputs):
        wanted, neighbours, own_pos, counts = inputs
        lookup = hidden[owners, wanted].reshape(N_DOM * R1, H)
        own_rows = jnp.take(lookup, own_pos, axis=0)
        mean_rows = average(lookup, neighbours, counts)
        joined = jnp.concatenate([own_rows, mean_rows], 1)
        return jnp.dot(joined, weight_two, preferred_element_type=jnp.float32).astype(jnp.bfloat16)

    seeds = lax.map(layer_two, (jnp.swapaxes(want_hid, 0, 1), nbr_hid.reshape(N_DOM, T2, FAN2), self_hid.reshape(N_DOM, T2), count_hid.reshape(N_DOM, T2)))
    return seeds.reshape(N_DOM * T2, H)
```

```python
import functools
import math

import jax
import jax.numpy as jnp
from jax import lax
from jax.experimental import pallas as pl
from jax.experimental.pallas import tpu as pltpu
from jax.sharding import PartitionSpec as P

F32 = jnp.float32
BF16 = jnp.bfloat16
I32 = jnp.int32
BLOCK = 256


def product(a, b):
    return jnp.dot(a, b, preferred_element_type=F32)


def tally(spots, first, last, block, weight=None):
    shifted = (spots - (block * BLOCK).astype(F32)).astype(BF16)
    lanes = lax.broadcasted_iota(I32, (spots.shape[0], BLOCK), 1).astype(F32).astype(BF16)
    one, none = jnp.ones((), BF16), jnp.zeros((), BF16)
    total = jnp.zeros(lanes.shape, BF16)
    for column in range(first, last):
        hit = jnp.broadcast_to(shifted[:, column : column + 1], lanes.shape) == lanes
        total = total + jnp.where(hit, one if weight is None else weight, none)
    return total


def kernel(
    shape,
    want_in, want_hid, store, nbr_in, self_in, count_in, w_one, nbr_hid, self_hid, count_hid, w_two,
    out,
    storef, nodes, table, picked, fetched, w_first, w_second, hidden, first_c, full, rows, seeds, second_c,
    local_sem, w_send, w_recv, f_send, f_recv, fc_send, fc_recv, h_send, h_recv, g_send, g_recv,
):
    doms, fan_one, fan_two = shape
    me, h, w = lax.axis_index("dom"), lax.axis_index("hid"), lax.axis_index("wt")
    core = lax.rem(h, 2)
    mate = {"hid": h + 1 - 2 * core}
    side_h = lax.rem(h + 2, 4)
    side = {"hid": side_h}
    over = {"wt": 1 - w}

    def remote(src, dst, send, recv, where):
        return pltpu.make_async_remote_copy(
            src_ref=src, dst_ref=dst, send_sem=send, recv_sem=recv,
            device_id=where, device_id_type=pl.DeviceIdType.MESH,
        )

    barrier = pltpu.get_barrier_semaphore()
    for where in (mate, side, over):
        pl.semaphore_signal(barrier, inc=1, device_id=where, device_id_type=pl.DeviceIdType.MESH)

    @pl.loop(1, doms)
    def _(s):
        pl.semaphore_signal(
            barrier, inc=1, device_id={"dom": lax.rem(me + s, doms)}, device_id_type=pl.DeviceIdType.MESH
        )

    half, features = picked.shape[1], picked.shape[2]
    fetch = want_hid.shape[1]
    width = w_first.shape[2]

    @pl.loop(0, store.shape[0], step=256)
    def _(start):
        start = pl.multiple_of(start, 256)
        storef[pl.ds(start, 256), :] = store[pl.ds(start, 256), :].astype(F32)

    @pl.loop(0, doms)
    def _(p):
        @pl.loop(0, half, step=16)
        def _(start):
            start = pl.multiple_of(start, 16)
            got = [storef[pl.ds(want_in[p, core * half + start + i], 1), :] for i in range(16)]
            picked[p, pl.ds(start, 16), :] = jnp.concatenate(got, 0).astype(BF16)

    pl.semaphore_wait(barrier, doms + 2)

    def fetch_copy(s, q, p):
        return remote(picked.at[p], fetched.at[q, core], f_send.at[s], f_recv.at[s], {"dom": p})

    def pass_copy(q, c):
        return remote(fetched.at[q, c], fetched.at[q, c], fc_send.at[q], fc_recv.at[q], mate)

    @pl.loop(1, doms)
    def _(s):
        fetch_copy(s, me, lax.rem(me + s, doms)).start()

    fetched[me, core] = picked[me]
    pass_copy(me, core).start()

    their_columns = pl.ds(pl.multiple_of((1 - w) * width, width), width)
    my_columns = pl.ds(pl.multiple_of(w * width, width), width)
    one_copy = remote(w_one.at[:, their_columns], w_first.at[w], w_send.at[0], w_recv.at[0], over)
    two_copy = remote(w_two, w_second.at[w], w_send.at[1], w_recv.at[1], over)
    one_copy.start()
    two_copy.start()
    local_one = pltpu.make_async_copy(w_one.at[:, my_columns], w_first.at[w], local_sem.at[0])
    local_two = pltpu.make_async_copy(w_two, w_second.at[w], local_sem.at[1])
    local_one.start()
    local_two.start()

    def slots(neighbours, own, counts, fan, span):
        number = counts[:, span]
        order = lax.broadcasted_iota(I32, (fan, number.shape[1]), 0)
        valid = jnp.where(order < number, neighbours[:, span], -1)
        lines = [valid.astype(F32), own[:, span].astype(F32), number.astype(F32)]
        pad = -(fan + 2) % 8
        if pad:
            lines.append(jnp.zeros((pad, number.shape[1]), F32))
        return jnp.concatenate(lines, 0).T

    @pl.loop(0, nodes.shape[0], step=512)
    def _(start):
        span = pl.ds(pl.multiple_of(start, 512), 512)
        nodes[span, :] = slots(nbr_in, self_in, count_in, fan_one, span)

    @pl.loop(0, doms)
    def _(p):
        @pl.loop(0, fetch, step=8)
        def _(start):
            start = pl.multiple_of(start, 8)
            got = [nodes[pl.ds(want_hid[p, start + i], 1), :] for i in range(8)]
            table[pl.ds(pl.multiple_of(p * fetch, 8) + start, 8), :] = jnp.concatenate(got, 0)

    @pl.loop(0, seeds.shape[0], step=512)
    def _(start):
        span = pl.ds(pl.multiple_of(start, 512), 512)
        seeds[span, :] = slots(nbr_hid, self_hid, count_hid, fan_two, span)

    def lanes_of(block):
        return pl.ds(pl.multiple_of(block * BLOCK, BLOCK), BLOCK)

    looked = doms * fetched.shape[1] * half
    group = math.gcd(doms, 4)
    step_rows = group * fetch

    def count_nodes(start):
        @pl.loop(0, step_rows, step=64)
        def _(part):
            part = pl.multiple_of(part, 64)
            spots = table[pl.ds(start + part, 64), :]

            @pl.loop(0, looked // BLOCK)
            def _(block):
                first_c[pl.ds(part, 64), lanes_of(block)] = tally(spots, 0, fan_one, block)
                there = pl.ds(pl.multiple_of(looked + block * BLOCK, BLOCK), BLOCK)
                first_c[pl.ds(part, 64), there] = tally(spots, fan_one, fan_one + 1, block)

    known = rows.shape[0] // 2

    def count_seeds(first, last, base):
        @pl.loop(first, last, step=64)
        def _(part):
            part = pl.multiple_of(part, 64)
            spots = seeds[pl.ds(part, 64), :]
            number = spots[:, fan_two + 1 : fan_two + 2].astype(BF16)

            @pl.loop(0, known // BLOCK)
            def _(block):
                there = pl.ds(pl.multiple_of(known + block * BLOCK, BLOCK), BLOCK)
                second_c[pl.ds(part - base, 64), lanes_of(block)] = tally(
                    spots, fan_two, fan_two + 1, block, number
                )
                second_c[pl.ds(part - base, 64), there] = tally(spots, 0, fan_two, block)

    small = doms == group
    total_seeds = seeds.shape[0]
    early = total_seeds // 2
    if small:
        count_nodes(0)

    @pl.loop(1, doms)
    def _(s):
        q = lax.rem(me - s + doms, doms)
        fetch_copy(s, q, lax.rem(me + s, doms)).wait_recv()
        pass_copy(q, core).start()

    if small:
        count_seeds(0, early, 0)

    @pl.loop(0, doms)
    def _(q):
        pass_copy(q, 1 - core).wait_recv()

    local_one.wait()
    one_copy.wait_recv()

    @pl.loop(0, doms // group)
    def _(part):
        start = pl.multiple_of(part * step_rows, step_rows)
        if not small:
            count_nodes(start)
        lookup = fetched[...].reshape(looked, features)
        number = table[pl.ds(start, step_rows), fan_one + 1 : fan_one + 2]
        mean = (product(first_c[:, :looked], lookup) / number).astype(BF16)
        own = product(first_c[:, looked:], lookup).astype(BF16)
        made = product(own, w_first[0]) + product(mean, w_first[1])
        made = jnp.maximum(made, 0.0).astype(BF16)
        for i in range(group):
            hidden[part * group + i] = made[i * fetch : (i + 1) * fetch]

    def columns_of(hh, ww):
        return pl.ds(pl.multiple_of((hh * 2 + ww) * width, width), width)

    mine, beside, across = columns_of(h, w), columns_of(side_h, w), columns_of(h, 1 - w)
    corner = columns_of(side_h, 1 - w)
    mate_h = h + 1 - 2 * core
    mate_side = lax.rem(mate_h + 2, 4)
    theirs = [
        columns_of(mate_h, w), columns_of(mate_side, w), columns_of(mate_h, 1 - w), columns_of(mate_side, 1 - w)
    ]

    def hidden_copy(s, q, p):
        return remote(hidden.at[p], full.at[q, :, mine], h_send.at[s], h_recv.at[s], {"dom": p})

    def plane(q, k, view, where):
        return remote(full.at[q, view[0], view[1]], full.at[q, view[0], view[1]], g_send.at[q, k], g_recv.at[q, k], where)

    everything, upper, lower = pl.ds(0, fetch), pl.ds(0, fetch // 2), pl.ds(fetch // 2, fetch // 2)

    def spread(q):
        plane(q, 0, (everything, mine), side).start()
        plane(q, 1, (everything, mine), over).start()
        plane(q, 4, (everything, mine), mate).start()

    @pl.loop(1, doms)
    def _(s):
        hidden_copy(s, me, lax.rem(me + s, doms)).start()

    full[me, :, mine] = hidden[me]
    spread(me)

    @pl.loop(1, doms)
    def _(s):
        q = lax.rem(me - s + doms, doms)
        hidden_copy(s, q, lax.rem(me + s, doms)).wait_recv()
        spread(q)

    @pl.loop(0, doms)
    def _(s):
        q = lax.rem(me - s + doms, doms)
        plane(q, 0, (everything, beside), side).wait_recv()
        plane(q, 2, (upper, beside), over).start()
        plane(q, 5, (everything, beside), mate).start()
        plane(q, 1, (everything, across), over).wait_recv()
        plane(q, 3, (lower, across), side).start()
        plane(q, 6, (everything, across), mate).start()

    if small:
        count_seeds(early, total_seeds, 0)

    @pl.loop(0, doms)
    def _(s):
        q = lax.rem(me - s + doms, doms)
        plane(q, 2, (upper, corner), over).wait_recv()
        plane(q, 3, (lower, corner), side).wait_recv()
        plane(q, 7, (everything, corner), mate).start()

    local_two.wait()
    two_copy.wait_recv()

    @pl.loop(0, doms)
    def _(s):
        q = lax.rem(me - s + doms, doms)
        for k in range(4):
            plane(q, 4 + k, (everything, theirs[k]), mate).wait_recv()

    @pl.loop(0, doms // group)
    def _(part):
        block = full[pl.ds(part * group, group)].reshape(step_rows, full.shape[2])
        start = pl.multiple_of(part * step_rows, step_rows)
        rows[pl.ds(start, step_rows), :] = product(block, w_second[0]).astype(BF16)
        rows[pl.ds(known + start, step_rows), :] = product(block, w_second[1]).astype(BF16)

    @pl.loop(0, total_seeds, step=256)
    def _(start):
        start = pl.multiple_of(start, 256)
        if small:
            counted = second_c[pl.ds(start, 256), :]
        else:
            count_seeds(start, start + 256, start)
            counted = second_c[...]
        number = seeds[pl.ds(start, 256), fan_two + 1 : fan_two + 2]
        out[pl.ds(start, 256), :] = (product(counted, rows[...]) / number).astype(BF16)

    one_copy.wait_send()
    two_copy.wait_send()

    @pl.loop(1, doms)
    def _(s):
        p = lax.rem(me + s, doms)
        fetch_copy(s, me, p).wait_send()
        hidden_copy(s, me, p).wait_send()

    @pl.loop(0, doms)
    def _(q):
        pass_copy(q, core).wait_send()
        plane(q, 0, (everything, mine), side).wait_send()
        plane(q, 1, (everything, mine), over).wait_send()
        plane(q, 2, (upper, beside), over).wait_send()
        plane(q, 3, (lower, across), side).wait_send()
        plane(q, 4, (everything, mine), mate).wait_send()
        plane(q, 5, (everything, beside), mate).wait_send()
        plane(q, 6, (everything, across), mate).wait_send()
        plane(q, 7, (everything, corner), mate).wait_send()


def shards(
    doms,
    store_feat,
    want_in,
    nbr_in,
    self_in,
    count_in,
    weight_one,
    want_hid,
    nbr_hid,
    self_hid,
    count_hid,
    weight_two,
):
    stored, features = store_feat.shape
    r0, r1 = want_in.shape[2], want_hid.shape[2]
    t1, fan_one = nbr_in.shape
    t2, fan_two = nbr_hid.shape
    width = weight_one.shape[1] // 2
    columns = weight_two.shape[1]
    group = math.gcd(doms, 4)
    known = doms * r1
    counted = t2 if doms == group else 256

    def padded(fan):
        return fan + 2 + -(fan + 2) % 8

    vmem = pl.BlockSpec(memory_space=pltpu.VMEM)
    smem = pl.BlockSpec(memory_space=pltpu.SMEM)
    dma = pltpu.SemaphoreType.DMA
    return pl.pallas_call(
        functools.partial(kernel, (doms, fan_one, fan_two)),
        out_shape=jax.ShapeDtypeStruct((t2, columns), BF16),
        in_specs=[smem, smem] + [vmem] * 9,
        out_specs=vmem,
        scratch_shapes=[
            pltpu.VMEM((stored, features), F32),
            pltpu.VMEM((t1, padded(fan_one)), F32),
            pltpu.VMEM((doms * r1, padded(fan_one)), F32),
            pltpu.VMEM((doms, r0 // 2, features), BF16),
            pltpu.VMEM((doms, 2, r0 // 2, features), BF16),
            pltpu.VMEM((2, features, width), BF16),
            pltpu.VMEM((2,) + weight_two.shape, BF16),
            pltpu.VMEM((doms, r1, width), BF16),
            pltpu.VMEM((group * r1, 2 * doms * r0), BF16),
            pltpu.VMEM((doms, r1, weight_two.shape[0]), BF16),
            pltpu.VMEM((2 * known, columns), BF16),
            pltpu.VMEM((t2, padded(fan_two)), F32),
            pltpu.VMEM((counted, 2 * known), BF16),
            dma((2,)), dma((2,)), dma((2,)),
            dma((doms,)), dma((doms,)), dma((doms,)), dma((doms,)), dma((doms,)), dma((doms,)),
            dma((doms, 8)), dma((doms, 8)),
        ],
        compiler_params=pltpu.CompilerParams(
            collective_id=0, has_side_effects=True, vmem_limit_bytes=56 << 20
        ),
    )(
        want_in[0], want_hid[0], store_feat, nbr_in.T, self_in[None], count_in[None], weight_one,
        nbr_hid.T, self_hid[None], count_hid[None], weight_two,
    )


def solution(mesh):
    return jax.shard_map(
        functools.partial(shards, mesh.shape["dom"]),
        mesh=mesh,
        in_specs=(
            P("dom", None),
            P("dom", None, None),
            P("dom", None),
            P("dom"),
            P("dom"),
            P("wt", "hid"),
            P("dom", None, None),
            P("dom", None),
            P("dom"),
            P("dom"),
            P("wt", "hid"),
        ),
        out_specs=P("dom", "hid"),
        check_vma=False,
    )
```

```python
import functools
import math

import jax
import jax.numpy as jnp
from jax import lax
from jax.experimental import pallas as pl
from jax.experimental.pallas import tpu as pltpu
from jax.sharding import PartitionSpec as P

F32 = jnp.float32
BF16 = jnp.bfloat16
I32 = jnp.int32
BLOCK = 256


def product(a, b):
    return jnp.dot(a, b, preferred_element_type=F32)


def turned_product(a, b):
    return lax.dot_general(a, b, (((0,), (0,)), ((), ())), preferred_element_type=F32)


def tally(spots, first, last, block, weight=None):
    shifted = (spots - (block * BLOCK).astype(F32)).astype(BF16)
    shape = (BLOCK, spots.shape[1])
    lines = lax.broadcasted_iota(I32, shape, 0).astype(F32).astype(BF16)
    none = jnp.zeros((), BF16)
    one = jnp.ones((), BF16) if weight is None else jnp.broadcast_to(weight, shape)
    total = jnp.zeros(shape, BF16)
    for slot in range(first, last):
        hit = jnp.broadcast_to(shifted[slot : slot + 1], shape) == lines
        total = total + jnp.where(hit, one, none)
    return total


def kernel(
    shape,
    want_in, want_hid, store, nbr_in, self_in, count_in, w_one, nbr_hid, self_hid, count_hid, w_two,
    out,
    storef, nodes, table, picked, fetched, w_first, w_second, hidden, first_c, full, rows, seeds, seed_count, second_c,
    local_sem, w_send, w_recv, f_send, f_recv, fc_send, fc_recv, h_send, h_recv, g_send, g_recv,
):
    doms, fan_one, fan_two = shape
    me, h, w = lax.axis_index("dom"), lax.axis_index("hid"), lax.axis_index("wt")
    core = lax.rem(h, 2)
    mate = {"hid": h + 1 - 2 * core}
    side_h = lax.rem(h + 2, 4)
    side = {"hid": side_h}
    over = {"wt": 1 - w}

    def remote(src, dst, send, recv, where):
        return pltpu.make_async_remote_copy(
            src_ref=src, dst_ref=dst, send_sem=send, recv_sem=recv,
            device_id=where, device_id_type=pl.DeviceIdType.MESH,
        )

    barrier = pltpu.get_barrier_semaphore()
    for where in (mate, side, over):
        pl.semaphore_signal(barrier, inc=1, device_id=where, device_id_type=pl.DeviceIdType.MESH)

    @pl.loop(1, doms)
    def _(s):
        pl.semaphore_signal(
            barrier, inc=1, device_id={"dom": lax.rem(me + s, doms)}, device_id_type=pl.DeviceIdType.MESH
        )

    half, features = picked.shape[1], picked.shape[2]
    fetch = want_hid.shape[1]
    width = w_first.shape[2]

    @pl.loop(0, store.shape[0], step=256)
    def _(start):
        start = pl.multiple_of(start, 256)
        storef[pl.ds(start, 256), :] = store[pl.ds(start, 256), :].astype(F32)

    @pl.loop(0, doms)
    def _(p):
        @pl.loop(0, half, step=16)
        def _(start):
            start = pl.multiple_of(start, 16)
            got = [storef[pl.ds(want_in[p, core * half + start + i], 1), :] for i in range(16)]
            picked[p, pl.ds(start, 16), :] = jnp.concatenate(got, 0).astype(BF16)

    pl.semaphore_wait(barrier, doms + 2)

    def fetch_copy(s, q, p):
        return remote(picked.at[p], fetched.at[q, core], f_send.at[s], f_recv.at[s], {"dom": p})

    def pass_copy(q, c):
        return remote(fetched.at[q, c], fetched.at[q, c], fc_send.at[q], fc_recv.at[q], mate)

    @pl.loop(1, doms)
    def _(s):
        fetch_copy(s, me, lax.rem(me + s, doms)).start()

    fetched[me, core] = picked[me]
    pass_copy(me, core).start()

    their_columns = pl.ds(pl.multiple_of((1 - w) * width, width), width)
    my_columns = pl.ds(pl.multiple_of(w * width, width), width)
    one_copy = remote(w_one.at[:, their_columns], w_first.at[w], w_send.at[0], w_recv.at[0], over)
    two_copy = remote(w_two, w_second.at[w], w_send.at[1], w_recv.at[1], over)
    one_copy.start()
    two_copy.start()
    local_one = pltpu.make_async_copy(w_one.at[:, my_columns], w_first.at[w], local_sem.at[0])
    local_two = pltpu.make_async_copy(w_two, w_second.at[w], local_sem.at[1])
    local_one.start()
    local_two.start()

    def slots(neighbours, own, counts, fan, span):
        number = counts[:, span]
        order = lax.broadcasted_iota(I32, (fan, number.shape[1]), 0)
        valid = jnp.where(order < number, neighbours[:, span], -1)
        lines = [valid.astype(F32), own[:, span].astype(F32), number.astype(F32)]
        pad = -(fan + 2) % 8
        if pad:
            lines.append(jnp.zeros((pad, number.shape[1]), F32))
        return jnp.concatenate(lines, 0)

    @pl.loop(0, nodes.shape[0], step=512)
    def _(start):
        span = pl.ds(pl.multiple_of(start, 512), 512)
        nodes[span, :] = slots(nbr_in, self_in, count_in, fan_one, span).T

    @pl.loop(0, doms)
    def _(p):
        @pl.loop(0, fetch, step=8)
        def _(start):
            start = pl.multiple_of(start, 8)
            for i in range(8):
                table[pl.ds(p * fetch + start + i, 1), :] = nodes[pl.ds(want_hid[p, start + i], 1), :]

    @pl.loop(0, seeds.shape[1], step=512)
    def _(start):
        span = pl.ds(pl.multiple_of(start, 512), 512)
        seeds[:, span] = slots(nbr_hid, self_hid, count_hid, fan_two, span)
        number = jnp.broadcast_to(count_hid[:, span].astype(F32), (8, 512))
        seed_count[span, :] = 1.0 / number.T

    def lines_of(block, base=0):
        return pl.ds(pl.multiple_of(base + block * BLOCK, BLOCK), BLOCK)

    looked = doms * fetched.shape[1] * half
    group = math.gcd(doms, 4)
    step_rows = group * fetch

    def count_nodes(start):
        @pl.loop(0, step_rows, step=128)
        def _(part):
            part = pl.multiple_of(part, 128)
            spots = table[pl.ds(start + part, 128), :].T

            @pl.loop(0, looked // BLOCK)
            def _(block):
                first_c[lines_of(block), pl.ds(part, 128)] = tally(spots, 0, fan_one, block)
                first_c[lines_of(block, looked), pl.ds(part, 128)] = tally(
                    spots, fan_one, fan_one + 1, block
                )

    known = rows.shape[0] // 2

    def count_seeds(first, last, base=0):
        @pl.loop(first, last, step=128)
        def _(part):
            part = pl.multiple_of(part, 128)
            spots = seeds[:, pl.ds(part, 128)]
            number = spots[fan_two + 1 : fan_two + 2].astype(BF16)
            span = pl.ds(pl.multiple_of(part - base, 128), 128)

            @pl.loop(0, known // BLOCK)
            def _(block):
                second_c[lines_of(block), span] = tally(spots, fan_two, fan_two + 1, block, number)
                second_c[lines_of(block, known), span] = tally(spots, 0, fan_two, block)

    small = doms == group
    total_seeds = seeds.shape[1]
    share = total_seeds // (2 * doms * 128) * 128
    early = share * (2 * doms - 1)
    if small:
        count_nodes(0)

    @pl.loop(1, doms)
    def _(s):
        q = lax.rem(me - s + doms, doms)
        fetch_copy(s, q, lax.rem(me + s, doms)).wait_recv()
        pass_copy(q, core).start()

    @pl.loop(0, doms)
    def _(q):
        pass_copy(q, 1 - core).wait_recv()

    local_one.wait()
    one_copy.wait_recv()

    @pl.loop(0, doms // group)
    def _(part):
        start = pl.multiple_of(part * step_rows, step_rows)
        if not small:
            count_nodes(start)
        lookup = fetched[...].reshape(looked, features)
        number = table[pl.ds(start, step_rows), fan_one + 1 : fan_one + 2]
        mean = (turned_product(first_c[:looked], lookup) / number).astype(BF16)
        own = turned_product(first_c[looked:], lookup).astype(BF16)
        made = product(own, w_first[0]) + product(mean, w_first[1])
        made = jnp.maximum(made, 0.0).astype(BF16)
        for i in range(group):
            hidden[part * group + i] = made[i * fetch : (i + 1) * fetch]

    def columns_of(hh, ww):
        return pl.ds(pl.multiple_of((hh * 2 + ww) * width, width), width)

    mine, beside, across = columns_of(h, w), columns_of(side_h, w), columns_of(h, 1 - w)
    corner = columns_of(side_h, 1 - w)
    mate_h = h + 1 - 2 * core
    mate_side = lax.rem(mate_h + 2, 4)
    theirs = [
        columns_of(mate_h, w), columns_of(mate_side, w), columns_of(mate_h, 1 - w), columns_of(mate_side, 1 - w)
    ]

    def hidden_copy(s, q, p):
        return remote(hidden.at[p], full.at[q, :, mine], h_send.at[s], h_recv.at[s], {"dom": p})

    def plane(q, k, view, where):
        return remote(full.at[q, view[0], view[1]], full.at[q, view[0], view[1]], g_send.at[q, k], g_recv.at[q, k], where)

    everything, upper, lower = pl.ds(0, fetch), pl.ds(0, fetch // 2), pl.ds(fetch // 2, fetch // 2)

    def spread(q):
        plane(q, 0, (everything, mine), side).start()
        plane(q, 1, (everything, mine), over).start()
        plane(q, 4, (everything, mine), mate).start()

    @pl.loop(1, doms)
    def _(s):
        hidden_copy(s, me, lax.rem(me + s, doms)).start()

    full[me, :, mine] = hidden[me]
    spread(me)

    @pl.loop(1, doms)
    def _(s):
        if small:
            count_seeds((s - 1) * share, s * share)
        q = lax.rem(me - s + doms, doms)
        hidden_copy(s, q, lax.rem(me + s, doms)).wait_recv()
        spread(q)

    @pl.loop(0, doms)
    def _(s):
        if small:
            count_seeds((doms - 1 + s) * share, (doms + s) * share)
        q = lax.rem(me - s + doms, doms)
        plane(q, 0, (everything, beside), side).wait_recv()
        plane(q, 2, (upper, beside), over).start()
        plane(q, 5, (everything, beside), mate).start()
        plane(q, 1, (everything, across), over).wait_recv()
        plane(q, 3, (lower, across), side).start()
        plane(q, 6, (everything, across), mate).start()

    if small:
        count_seeds(early, total_seeds)

    @pl.loop(0, doms)
    def _(s):
        q = lax.rem(me - s + doms, doms)
        plane(q, 2, (upper, corner), over).wait_recv()
        plane(q, 3, (lower, corner), side).wait_recv()
        plane(q, 7, (everything, corner), mate).start()

    local_two.wait()
    two_copy.wait_recv()

    @pl.loop(0, doms)
    def _(s):
        q = lax.rem(me - s + doms, doms)
        for k in range(4):
            plane(q, 4 + k, (everything, theirs[k]), mate).wait_recv()

    @pl.loop(0, doms // group)
    def _(part):
        block = full[pl.ds(part * group, group)].reshape(step_rows, full.shape[2])
        start = pl.multiple_of(part * step_rows, step_rows)
        rows[pl.ds(start, step_rows), :] = product(block, w_second[0]).astype(BF16)
        rows[pl.ds(known + start, step_rows), :] = product(block, w_second[1]).astype(BF16)

    chunk = 512 if small else second_c.shape[1]

    @pl.loop(0, total_seeds, step=chunk)
    def _(start):
        start = pl.multiple_of(start, chunk)
        if small:
            counted = second_c[:, pl.ds(start, chunk)]
        else:
            count_seeds(start, start + chunk, start)
            counted = second_c[...]
        share_of_one = seed_count[pl.ds(start, chunk), :1]
        out[pl.ds(start, chunk), :] = (turned_product(counted, rows[...]) * share_of_one).astype(BF16)

    one_copy.wait_send()
    two_copy.wait_send()

    @pl.loop(1, doms)
    def _(s):
        p = lax.rem(me + s, doms)
        fetch_copy(s, me, p).wait_send()
        hidden_copy(s, me, p).wait_send()

    @pl.loop(0, doms)
    def _(q):
        pass_copy(q, core).wait_send()
        plane(q, 0, (everything, mine), side).wait_send()
        plane(q, 1, (everything, mine), over).wait_send()
        plane(q, 2, (upper, beside), over).wait_send()
        plane(q, 3, (lower, across), side).wait_send()
        plane(q, 4, (everything, mine), mate).wait_send()
        plane(q, 5, (everything, beside), mate).wait_send()
        plane(q, 6, (everything, across), mate).wait_send()
        plane(q, 7, (everything, corner), mate).wait_send()


def shards(
    doms,
    store_feat,
    want_in,
    nbr_in,
    self_in,
    count_in,
    weight_one,
    want_hid,
    nbr_hid,
    self_hid,
    count_hid,
    weight_two,
):
    stored, features = store_feat.shape
    r0, r1 = want_in.shape[2], want_hid.shape[2]
    t1, fan_one = nbr_in.shape
    t2, fan_two = nbr_hid.shape
    width = weight_one.shape[1] // 2
    columns = weight_two.shape[1]
    group = math.gcd(doms, 4)
    known = doms * r1
    counted = t2 if doms == group else 256

    def padded(fan):
        return fan + 2 + -(fan + 2) % 8

    vmem = pl.BlockSpec(memory_space=pltpu.VMEM)
    smem = pl.BlockSpec(memory_space=pltpu.SMEM)
    dma = pltpu.SemaphoreType.DMA
    return pl.pallas_call(
        functools.partial(kernel, (doms, fan_one, fan_two)),
        out_shape=jax.ShapeDtypeStruct((t2, columns), BF16),
        in_specs=[smem, smem] + [vmem] * 9,
        out_specs=vmem,
        scratch_shapes=[
            pltpu.VMEM((stored, features), F32),
            pltpu.VMEM((t1, padded(fan_one)), F32),
            pltpu.VMEM((doms * r1, padded(fan_one)), F32),
            pltpu.VMEM((doms, r0 // 2, features), BF16),
            pltpu.VMEM((doms, 2, r0 // 2, features), BF16),
            pltpu.VMEM((2, features, width), BF16),
            pltpu.VMEM((2,) + weight_two.shape, BF16),
            pltpu.VMEM((doms, r1, width), BF16),
            pltpu.VMEM((2 * doms * r0, group * r1), BF16),
            pltpu.VMEM((doms, r1, weight_two.shape[0]), BF16),
            pltpu.VMEM((2 * known, columns), BF16),
            pltpu.VMEM((padded(fan_two), t2), F32),
            pltpu.VMEM((t2, 8), F32),
            pltpu.VMEM((2 * known, counted), BF16),
            dma((2,)), dma((2,)), dma((2,)),
            dma((doms,)), dma((doms,)), dma((doms,)), dma((doms,)), dma((doms,)), dma((doms,)),
            dma((doms, 8)), dma((doms, 8)),
        ],
        compiler_params=pltpu.CompilerParams(
            collective_id=0, has_side_effects=True, vmem_limit_bytes=56 << 20
        ),
    )(
        want_in[0], want_hid[0], store_feat, nbr_in.T, self_in[None], count_in[None], weight_one,
        nbr_hid.T, self_hid[None], count_hid[None], weight_two,
    )


def solution(mesh):
    return jax.shard_map(
        functools.partial(shards, mesh.shape["dom"]),
        mesh=mesh,
        in_specs=(
            P("dom", None),
            P("dom", None, None),
            P("dom", None),
            P("dom"),
            P("dom"),
            P("wt", "hid"),
            P("dom", None, None),
            P("dom", None),
            P("dom"),
            P("dom"),
            P("wt", "hid"),
        ),
        out_specs=P("dom", "hid"),
        check_vma=False,
    )
```

```python
import functools
import math

import jax
import jax.numpy as jnp
from jax import lax
from jax.experimental import pallas as pl
from jax.experimental.pallas import tpu as pltpu
from jax.sharding import PartitionSpec as P

F32 = jnp.float32
BF16 = jnp.bfloat16
I32 = jnp.int32
BLOCK = 256


def product(a, b):
    return jnp.dot(a, b, preferred_element_type=F32)


def turned_product(a, b):
    return lax.dot_general(a, b, (((0,), (0,)), ((), ())), preferred_element_type=F32)


def tally(spots, first, last, block, weight=None):
    shifted = (spots - (block * BLOCK).astype(F32)).astype(BF16)
    shape = (BLOCK, spots.shape[1])
    lines = lax.broadcasted_iota(I32, shape, 0).astype(F32).astype(BF16)
    none = jnp.zeros((), BF16)
    one = jnp.ones((), BF16) if weight is None else jnp.broadcast_to(weight, shape)
    total = jnp.zeros(shape, BF16)
    for slot in range(first, last):
        hit = jnp.broadcast_to(shifted[slot : slot + 1], shape) == lines
        total = total + jnp.where(hit, one, none)
    return total


def kernel(
    shape,
    want_in, want_hid, store, nbr_in, self_in, count_in, w_one, nbr_hid, self_hid, count_hid, w_two,
    out,
    storef, nodes, table, picked, fetched, w_first, w_second, hidden, first_c, full, rows, seeds, seed_count, second_c,
    local_sem, w_send, w_recv, f_send, f_recv, fc_send, fc_recv, h_send, h_recv, g_send, g_recv,
):
    doms, fan_one, fan_two = shape
    me, h, w = lax.axis_index("dom"), lax.axis_index("hid"), lax.axis_index("wt")
    core = lax.rem(h, 2)
    mate = {"hid": h + 1 - 2 * core}
    side_h = lax.rem(h + 2, 4)
    side = {"hid": side_h}
    over = {"wt": 1 - w}

    def remote(src, dst, send, recv, where):
        return pltpu.make_async_remote_copy(
            src_ref=src, dst_ref=dst, send_sem=send, recv_sem=recv,
            device_id=where, device_id_type=pl.DeviceIdType.MESH,
        )

    barrier = pltpu.get_barrier_semaphore()
    for where in (mate, side, over):
        pl.semaphore_signal(barrier, inc=1, device_id=where, device_id_type=pl.DeviceIdType.MESH)

    @pl.loop(1, doms)
    def _(s):
        pl.semaphore_signal(
            barrier, inc=1, device_id={"dom": lax.rem(me + s, doms)}, device_id_type=pl.DeviceIdType.MESH
        )

    half, features = picked.shape[1], picked.shape[2]
    fetch = want_hid.shape[1]
    width = w_first.shape[2]

    @pl.loop(0, store.shape[0], step=256)
    def _(start):
        start = pl.multiple_of(start, 256)
        storef[pl.ds(start, 256), :] = store[pl.ds(start, 256), :].astype(F32)

    @pl.loop(0, doms)
    def _(p):
        @pl.loop(0, half, step=16)
        def _(start):
            start = pl.multiple_of(start, 16)
            got = [storef[pl.ds(want_in[p, core * half + start + i], 1), :] for i in range(16)]
            picked[p, pl.ds(start, 16), :] = jnp.concatenate(got, 0).astype(BF16)

    pl.semaphore_wait(barrier, doms + 2)

    def fetch_copy(s, q, p):
        return remote(picked.at[p], fetched.at[q, core], f_send.at[s], f_recv.at[s], {"dom": p})

    def pass_copy(q, c):
        return remote(fetched.at[q, c], fetched.at[q, c], fc_send.at[q], fc_recv.at[q], mate)

    @pl.loop(1, doms)
    def _(s):
        fetch_copy(s, me, lax.rem(me + s, doms)).start()

    fetched[me, core] = picked[me]
    pass_copy(me, core).start()

    their_columns = pl.ds(pl.multiple_of((1 - w) * width, width), width)
    my_columns = pl.ds(pl.multiple_of(w * width, width), width)
    one_copy = remote(w_one.at[:, their_columns], w_first.at[w], w_send.at[0], w_recv.at[0], over)
    two_copy = remote(w_two, w_second.at[w], w_send.at[1], w_recv.at[1], over)
    one_copy.start()
    two_copy.start()
    local_one = pltpu.make_async_copy(w_one.at[:, my_columns], w_first.at[w], local_sem.at[0])
    local_two = pltpu.make_async_copy(w_two, w_second.at[w], local_sem.at[1])
    local_one.start()
    local_two.start()

    def slots(neighbours, own, counts, fan, span):
        number = counts[:, span]
        order = lax.broadcasted_iota(I32, (fan, number.shape[1]), 0)
        valid = jnp.where(order < number, neighbours[:, span], -1)
        lines = [valid.astype(F32), own[:, span].astype(F32), number.astype(F32)]
        pad = -(fan + 2) % 8
        if pad:
            lines.append(jnp.zeros((pad, number.shape[1]), F32))
        return jnp.concatenate(lines, 0)

    @pl.loop(0, nodes.shape[0], step=512)
    def _(start):
        span = pl.ds(pl.multiple_of(start, 512), 512)
        nodes[span, :] = slots(nbr_in, self_in, count_in, fan_one, span).T

    @pl.loop(0, doms)
    def _(p):
        @pl.loop(0, fetch, step=8)
        def _(start):
            start = pl.multiple_of(start, 8)
            for i in range(8):
                table[pl.ds(p * fetch + start + i, 1), :] = nodes[pl.ds(want_hid[p, start + i], 1), :]

    @pl.loop(0, seeds.shape[1], step=512)
    def _(start):
        span = pl.ds(pl.multiple_of(start, 512), 512)
        seeds[:, span] = slots(nbr_hid, self_hid, count_hid, fan_two, span)
        number = jnp.broadcast_to(count_hid[:, span].astype(F32), (8, 512))
        seed_count[span, :] = 1.0 / number.T

    def lines_of(block, base=0):
        return pl.ds(pl.multiple_of(base + block * BLOCK, BLOCK), BLOCK)

    looked = doms * fetched.shape[1] * half
    group = math.gcd(doms, 4)
    step_rows = group * fetch

    def count_nodes(start):
        @pl.loop(0, step_rows, step=128)
        def _(part):
            part = pl.multiple_of(part, 128)
            spots = table[pl.ds(start + part, 128), :].T

            @pl.loop(0, looked // BLOCK)
            def _(block):
                first_c[lines_of(block), pl.ds(part, 128)] = tally(spots, 0, fan_one, block)
                first_c[lines_of(block, looked), pl.ds(part, 128)] = tally(
                    spots, fan_one, fan_one + 1, block
                )

    known = rows.shape[0] // 2

    def count_seeds(first, last, base=0):
        @pl.loop(first, last, step=128)
        def _(part):
            part = pl.multiple_of(part, 128)
            spots = seeds[:, pl.ds(part, 128)]
            number = spots[fan_two + 1 : fan_two + 2].astype(BF16)
            span = pl.ds(pl.multiple_of(part - base, 128), 128)

            @pl.loop(0, known // BLOCK)
            def _(block):
                second_c[lines_of(block), span] = tally(spots, fan_two, fan_two + 1, block, number)
                second_c[lines_of(block, known), span] = tally(spots, 0, fan_two, block)

    small = doms == group
    total_seeds = seeds.shape[1]
    share = total_seeds // (2 * doms * 128) * 128
    early = share * (2 * doms - 1)
    if small:
        count_nodes(0)

    @pl.loop(1, doms)
    def _(s):
        q = lax.rem(me - s + doms, doms)
        fetch_copy(s, q, lax.rem(me + s, doms)).wait_recv()
        pass_copy(q, core).start()

    @pl.loop(0, doms)
    def _(q):
        pass_copy(q, 1 - core).wait_recv()

    local_one.wait()
    one_copy.wait_recv()

    @pl.loop(0, doms // group)
    def _(part):
        start = pl.multiple_of(part * step_rows, step_rows)
        if not small:
            count_nodes(start)
        lookup = fetched[...].reshape(looked, features)
        number = table[pl.ds(start, step_rows), fan_one + 1 : fan_one + 2]
        mean = (turned_product(first_c[:looked], lookup) / number).astype(BF16)
        own = turned_product(first_c[looked:], lookup).astype(BF16)
        made = product(own, w_first[0]) + product(mean, w_first[1])
        made = jnp.maximum(made, 0.0).astype(BF16)
        for i in range(group):
            hidden[part * group + i] = made[i * fetch : (i + 1) * fetch]

    def columns_of(hh, ww):
        return pl.ds(pl.multiple_of((hh * 2 + ww) * width, width), width)

    mine, beside, across = columns_of(h, w), columns_of(side_h, w), columns_of(h, 1 - w)
    corner = columns_of(side_h, 1 - w)
    mate_h = h + 1 - 2 * core
    mate_side = lax.rem(mate_h + 2, 4)
    theirs = [
        columns_of(mate_h, w), columns_of(mate_side, w), columns_of(mate_h, 1 - w), columns_of(mate_side, 1 - w)
    ]

    def hidden_copy(s, q, p):
        return remote(hidden.at[p], full.at[q, :, mine], h_send.at[s], h_recv.at[s], {"dom": p})

    def plane(q, k, view, where):
        return remote(full.at[q, view[0], view[1]], full.at[q, view[0], view[1]], g_send.at[q, k], g_recv.at[q, k], where)

    everything, upper, lower = pl.ds(0, fetch), pl.ds(0, fetch // 2), pl.ds(fetch // 2, fetch // 2)

    def spread(q):
        plane(q, 0, (everything, mine), side).start()
        plane(q, 1, (everything, mine), over).start()
        plane(q, 4, (everything, mine), mate).start()

    @pl.loop(1, doms)
    def _(s):
        hidden_copy(s, me, lax.rem(me + s, doms)).start()

    full[me, :, mine] = hidden[me]
    spread(me)

    @pl.loop(1, doms)
    def _(s):
        if small:
            count_seeds((s - 1) * share, s * share)
        q = lax.rem(me - s + doms, doms)
        hidden_copy(s, q, lax.rem(me + s, doms)).wait_recv()
        spread(q)

    @pl.loop(0, doms)
    def _(s):
        if small:
            count_seeds((doms - 1 + s) * share, (doms + s) * share)
        q = lax.rem(me - s + doms, doms)
        plane(q, 0, (everything, beside), side).wait_recv()
        plane(q, 2, (upper, beside), over).start()
        plane(q, 5, (everything, beside), mate).start()
        plane(q, 1, (everything, across), over).wait_recv()
        plane(q, 3, (lower, across), side).start()
        plane(q, 6, (everything, across), mate).start()

    if small:
        count_seeds(early, total_seeds)
        keep_counts = pltpu.make_async_copy(second_c, out, local_sem.at[2])
        keep_counts.start()

    @pl.loop(0, doms)
    def _(s):
        q = lax.rem(me - s + doms, doms)
        plane(q, 2, (upper, corner), over).wait_recv()
        plane(q, 3, (lower, corner), side).wait_recv()
        plane(q, 7, (everything, corner), mate).start()

    local_two.wait()
    two_copy.wait_recv()

    @pl.loop(0, doms)
    def _(s):
        q = lax.rem(me - s + doms, doms)
        for k in range(4):
            plane(q, 4 + k, (everything, theirs[k]), mate).wait_recv()

    @pl.loop(0, doms // group)
    def _(part):
        block = full[pl.ds(part * group, group)].reshape(step_rows, full.shape[2])
        start = pl.multiple_of(part * step_rows, step_rows)
        rows[pl.ds(start, step_rows), :] = product(block, w_second[0]).astype(BF16)
        rows[pl.ds(known + start, step_rows), :] = product(block, w_second[1]).astype(BF16)

    if not small:
        chunk = second_c.shape[1]

        @pl.loop(0, total_seeds, step=chunk)
        def _(start):
            start = pl.multiple_of(start, chunk)
            count_seeds(start, start + chunk, start)
            made = turned_product(second_c[...], rows[...]) * seed_count[pl.ds(start, chunk), :1]
            out[pl.ds(start, chunk), :] = made.astype(BF16)

    one_copy.wait_send()
    two_copy.wait_send()

    @pl.loop(1, doms)
    def _(s):
        p = lax.rem(me + s, doms)
        fetch_copy(s, me, p).wait_send()
        hidden_copy(s, me, p).wait_send()

    @pl.loop(0, doms)
    def _(q):
        pass_copy(q, core).wait_send()
        plane(q, 0, (everything, mine), side).wait_send()
        plane(q, 1, (everything, mine), over).wait_send()
        plane(q, 2, (upper, beside), over).wait_send()
        plane(q, 3, (lower, across), side).wait_send()
        plane(q, 4, (everything, mine), mate).wait_send()
        plane(q, 5, (everything, beside), mate).wait_send()
        plane(q, 6, (everything, across), mate).wait_send()
        plane(q, 7, (everything, corner), mate).wait_send()

    if small:
        keep_counts.wait()


def split_kernel(shape, *refs):
    inputs, (rows, seed_count, counts), rest = refs[:11], refs[11:14], refs[14:]
    kernel(shape, *inputs, counts, *rest[:10], rows, rest[10], seed_count, *rest[11:])


def seed_kernel(counts, rows, seed_count, out):
    out[...] = (turned_product(counts[...], rows[...]) * seed_count[:, :1]).astype(BF16)


def shards(
    doms,
    store_feat,
    want_in,
    nbr_in,
    self_in,
    count_in,
    weight_one,
    want_hid,
    nbr_hid,
    self_hid,
    count_hid,
    weight_two,
):
    stored, features = store_feat.shape
    r0, r1 = want_in.shape[2], want_hid.shape[2]
    t1, fan_one = nbr_in.shape
    t2, fan_two = nbr_hid.shape
    width = weight_one.shape[1] // 2
    columns = weight_two.shape[1]
    group = math.gcd(doms, 4)
    known = doms * r1
    counted = t2 if doms == group else 256

    def padded(fan):
        return fan + 2 + -(fan + 2) % 8

    vmem = pl.BlockSpec(memory_space=pltpu.VMEM)
    smem = pl.BlockSpec(memory_space=pltpu.SMEM)
    dma = pltpu.SemaphoreType.DMA
    small = doms == group
    scratch = [
        pltpu.VMEM((stored, features), F32),
        pltpu.VMEM((t1, padded(fan_one)), F32),
        pltpu.VMEM((doms * r1, padded(fan_one)), F32),
        pltpu.VMEM((doms, r0 // 2, features), BF16),
        pltpu.VMEM((doms, 2, r0 // 2, features), BF16),
        pltpu.VMEM((2, features, width), BF16),
        pltpu.VMEM((2,) + weight_two.shape, BF16),
        pltpu.VMEM((doms, r1, width), BF16),
        pltpu.VMEM((2 * doms * r0, group * r1), BF16),
        pltpu.VMEM((doms, r1, weight_two.shape[0]), BF16),
        pltpu.VMEM((2 * known, columns), BF16),
        pltpu.VMEM((padded(fan_two), t2), F32),
        pltpu.VMEM((t2, 8), F32),
        pltpu.VMEM((2 * known, counted), BF16),
        dma((3,)), dma((2,)), dma((2,)),
        dma((doms,)), dma((doms,)), dma((doms,)), dma((doms,)), dma((doms,)), dma((doms,)),
        dma((doms, 8)), dma((doms, 8)),
    ]
    result = jax.ShapeDtypeStruct((t2, columns), BF16)
    results, places = result, vmem
    if small:
        seed_count, rows = scratch.pop(12), scratch.pop(10)
        results = (
            jax.ShapeDtypeStruct(rows.shape, BF16),
            jax.ShapeDtypeStruct(seed_count.shape, F32),
            jax.ShapeDtypeStruct((2 * known, t2), BF16),
        )
        places = (vmem, vmem, pl.BlockSpec(memory_space=pl.ANY))
    made = pl.pallas_call(
        functools.partial(split_kernel if small else kernel, (doms, fan_one, fan_two)),
        out_shape=results,
        in_specs=[smem, smem] + [vmem] * 9,
        out_specs=places,
        scratch_shapes=scratch,
        compiler_params=pltpu.CompilerParams(
            collective_id=0, has_side_effects=True, vmem_limit_bytes=56 << 20
        ),
    )(
        want_in[0], want_hid[0], store_feat, nbr_in.T, self_in[None], count_in[None], weight_one,
        nbr_hid.T, self_hid[None], count_hid[None], weight_two,
    )
    if not small:
        return made
    rows, seed_count, counts = made
    chunk = math.gcd(t2, 512)
    return pl.pallas_call(
        seed_kernel,
        out_shape=result,
        grid=(t2 // chunk,),
        in_specs=[
            pl.BlockSpec((2 * known, chunk), lambda i: (0, i)),
            pl.BlockSpec((2 * known, columns), lambda i: (0, 0)),
            pl.BlockSpec((chunk, 8), lambda i: (i, 0)),
        ],
        out_specs=pl.BlockSpec((chunk, columns), lambda i: (i, 0)),
        compiler_params=pltpu.CompilerParams(vmem_limit_bytes=24 << 20),
    )(counts, rows, seed_count)


def solution(mesh):
    return jax.shard_map(
        functools.partial(shards, mesh.shape["dom"]),
        mesh=mesh,
        in_specs=(
            P("dom", None),
            P("dom", None, None),
            P("dom", None),
            P("dom"),
            P("dom"),
            P("wt", "hid"),
            P("dom", None, None),
            P("dom", None),
            P("dom"),
            P("dom"),
            P("wt", "hid"),
        ),
        out_specs=P("dom", "hid"),
        check_vma=False,
    )
```

```python
import functools
import math

import jax
import jax.numpy as jnp
from jax import lax
from jax.experimental import pallas as pl
from jax.experimental.pallas import tpu as pltpu
from jax.sharding import PartitionSpec as P

F32 = jnp.float32
BF16 = jnp.bfloat16
I32 = jnp.int32
BLOCK = 256


def product(a, b):
    return jnp.dot(a, b, preferred_element_type=F32)


def turned_product(a, b):
    return lax.dot_general(a, b, (((0,), (0,)), ((), ())), preferred_element_type=F32)


def tally(spots, first, last, block, weight=None):
    shifted = (spots - (block * BLOCK).astype(F32)).astype(BF16)
    shape = (BLOCK, spots.shape[1])
    lines = lax.broadcasted_iota(I32, shape, 0).astype(F32).astype(BF16)
    none = jnp.zeros((), BF16)
    one = jnp.ones((), BF16) if weight is None else jnp.broadcast_to(weight, shape)
    total = jnp.zeros(shape, BF16)
    for slot in range(first, last):
        hit = jnp.broadcast_to(shifted[slot : slot + 1], shape) == lines
        total = total + jnp.where(hit, one, none)
    return total


def kernel(
    shape,
    want_in, want_hid, store, nbr_in, self_in, count_in, w_one, nbr_hid, self_hid, count_hid, w_two,
    out,
    storef, nodes, table, picked, fetched, w_first, w_second, hidden, first_c, full, rows, seeds, seed_count, second_c,
    local_sem, w_send, w_recv, f_send, f_recv, fc_send, fc_recv, h_send, h_recv, g_send, g_recv,
):
    doms, fan_one, fan_two = shape
    me, h, w = lax.axis_index("dom"), lax.axis_index("hid"), lax.axis_index("wt")
    core = lax.rem(h, 2)
    mate = {"hid": h + 1 - 2 * core}
    side_h = lax.rem(h + 2, 4)
    side = {"hid": side_h}
    over = {"wt": 1 - w}

    def remote(src, dst, send, recv, where):
        return pltpu.make_async_remote_copy(
            src_ref=src, dst_ref=dst, send_sem=send, recv_sem=recv,
            device_id=where, device_id_type=pl.DeviceIdType.MESH,
        )

    barrier = pltpu.get_barrier_semaphore()
    for where in (mate, side, over):
        pl.semaphore_signal(barrier, inc=1, device_id=where, device_id_type=pl.DeviceIdType.MESH)

    @pl.loop(1, doms)
    def _(s):
        pl.semaphore_signal(
            barrier, inc=1, device_id={"dom": lax.rem(me + s, doms)}, device_id_type=pl.DeviceIdType.MESH
        )

    half, features = picked.shape[1], picked.shape[2]
    fetch = want_hid.shape[1]
    width = w_first.shape[2]

    @pl.loop(0, store.shape[0], step=256)
    def _(start):
        start = pl.multiple_of(start, 256)
        storef[pl.ds(start, 256), :] = store[pl.ds(start, 256), :].astype(F32)

    pl.semaphore_wait(barrier, doms + 2)

    their_columns = pl.ds(pl.multiple_of((1 - w) * width, width), width)
    my_columns = pl.ds(pl.multiple_of(w * width, width), width)
    one_copy = remote(w_one.at[:, their_columns], w_first.at[w], w_send.at[0], w_recv.at[0], over)
    two_copy = remote(w_two, w_second.at[w], w_send.at[1], w_recv.at[1], over)
    one_copy.start()
    two_copy.start()
    local_one = pltpu.make_async_copy(w_one.at[:, my_columns], w_first.at[w], local_sem.at[0])
    local_two = pltpu.make_async_copy(w_two, w_second.at[w], local_sem.at[1])
    local_one.start()
    local_two.start()

    @pl.loop(0, doms)
    def _(p):
        @pl.loop(0, half, step=16)
        def _(start):
            start = pl.multiple_of(start, 16)
            got = [storef[pl.ds(want_in[p, core * half + start + i], 1), :] for i in range(16)]
            picked[p, pl.ds(start, 16), :] = jnp.concatenate(got, 0).astype(BF16)

    def fetch_copy(s, q, p):
        return remote(picked.at[p], fetched.at[q, core], f_send.at[s], f_recv.at[s], {"dom": p})

    def pass_copy(q, c):
        return remote(fetched.at[q, c], fetched.at[q, c], fc_send.at[q], fc_recv.at[q], mate)

    @pl.loop(1, doms)
    def _(s):
        fetch_copy(s, me, lax.rem(me + s, doms)).start()

    fetched[me, core] = picked[me]
    pass_copy(me, core).start()

    def slots(neighbours, own, counts, fan, span):
        number = counts[:, span]
        order = lax.broadcasted_iota(I32, (fan, number.shape[1]), 0)
        valid = jnp.where(order < number, neighbours[:, span], -1)
        lines = [valid.astype(F32), own[:, span].astype(F32), number.astype(F32)]
        pad = -(fan + 2) % 8
        if pad:
            lines.append(jnp.zeros((pad, number.shape[1]), F32))
        return jnp.concatenate(lines, 0)

    @pl.loop(0, nodes.shape[0], step=512)
    def _(start):
        span = pl.ds(pl.multiple_of(start, 512), 512)
        nodes[span, :] = slots(nbr_in, self_in, count_in, fan_one, span).T

    @pl.loop(0, doms)
    def _(p):
        @pl.loop(0, fetch, step=8)
        def _(start):
            start = pl.multiple_of(start, 8)
            for i in range(8):
                table[pl.ds(p * fetch + start + i, 1), :] = nodes[pl.ds(want_hid[p, start + i], 1), :]

    @pl.loop(0, seeds.shape[1], step=512)
    def _(start):
        span = pl.ds(pl.multiple_of(start, 512), 512)
        seeds[:, span] = slots(nbr_hid, self_hid, count_hid, fan_two, span)
        number = jnp.broadcast_to(count_hid[:, span].astype(F32), (8, 512))
        seed_count[span, :] = 1.0 / number.T

    def lines_of(block, base=0):
        return pl.ds(pl.multiple_of(base + block * BLOCK, BLOCK), BLOCK)

    looked = doms * fetched.shape[1] * half
    group = math.gcd(doms, 4)
    step_rows = group * fetch

    def count_nodes(start):
        @pl.loop(0, step_rows, step=128)
        def _(part):
            part = pl.multiple_of(part, 128)
            spots = table[pl.ds(start + part, 128), :].T

            @pl.loop(0, looked // BLOCK)
            def _(block):
                first_c[lines_of(block), pl.ds(part, 128)] = tally(spots, 0, fan_one, block)
                first_c[lines_of(block, looked), pl.ds(part, 128)] = tally(
                    spots, fan_one, fan_one + 1, block
                )

    known = rows.shape[0] // 2

    def count_seeds(first, last, base=0):
        @pl.loop(first, last, step=128)
        def _(part):
            part = pl.multiple_of(part, 128)
            spots = seeds[:, pl.ds(part, 128)]
            number = spots[fan_two + 1 : fan_two + 2].astype(BF16)
            span = pl.ds(pl.multiple_of(part - base, 128), 128)

            @pl.loop(0, known // BLOCK)
            def _(block):
                second_c[lines_of(block), span] = tally(spots, fan_two, fan_two + 1, block, number)
                second_c[lines_of(block, known), span] = tally(spots, 0, fan_two, block)

    small = doms == group
    total_seeds = seeds.shape[1]
    share = total_seeds // (2 * doms * 128) * 128
    early = share * (2 * doms - 1)
    if small:
        count_nodes(0)

    @pl.loop(1, doms)
    def _(s):
        q = lax.rem(me - s + doms, doms)
        fetch_copy(s, q, lax.rem(me + s, doms)).wait_recv()
        pass_copy(q, core).start()

    @pl.loop(0, doms)
    def _(q):
        pass_copy(q, 1 - core).wait_recv()

    local_one.wait()
    one_copy.wait_recv()

    @pl.loop(0, doms // group)
    def _(part):
        start = pl.multiple_of(part * step_rows, step_rows)
        if not small:
            count_nodes(start)
        lookup = fetched[...].reshape(looked, features)
        number = table[pl.ds(start, step_rows), fan_one + 1 : fan_one + 2]
        mean = (turned_product(first_c[:looked], lookup) / number).astype(BF16)
        own = turned_product(first_c[looked:], lookup).astype(BF16)
        made = product(own, w_first[0]) + product(mean, w_first[1])
        made = jnp.maximum(made, 0.0).astype(BF16)
        for i in range(group):
            hidden[part * group + i] = made[i * fetch : (i + 1) * fetch]

    def columns_of(hh, ww):
        return pl.ds(pl.multiple_of((hh * 2 + ww) * width, width), width)

    mine, beside, across = columns_of(h, w), columns_of(side_h, w), columns_of(h, 1 - w)
    corner = columns_of(side_h, 1 - w)
    mate_h = h + 1 - 2 * core
    mate_side = lax.rem(mate_h + 2, 4)
    theirs = [
        columns_of(mate_h, w), columns_of(mate_side, w), columns_of(mate_h, 1 - w), columns_of(mate_side, 1 - w)
    ]

    def hidden_copy(s, q, p):
        return remote(hidden.at[p], full.at[q, :, mine], h_send.at[s], h_recv.at[s], {"dom": p})

    def plane(q, k, view, where):
        return remote(full.at[q, view[0], view[1]], full.at[q, view[0], view[1]], g_send.at[q, k], g_recv.at[q, k], where)

    everything = pl.ds(0, fetch)

    def spread(q):
        plane(q, 0, (everything, mine), side).start()
        plane(q, 1, (everything, mine), over).start()
        plane(q, 4, (everything, mine), mate).start()

    @pl.loop(1, doms)
    def _(s):
        hidden_copy(s, me, lax.rem(me + s, doms)).start()

    full[me, :, mine] = hidden[me]
    spread(me)

    @pl.loop(1, doms)
    def _(s):
        if small:
            count_seeds((s - 1) * share, s * share)
        q = lax.rem(me - s + doms, doms)
        hidden_copy(s, q, lax.rem(me + s, doms)).wait_recv()
        spread(q)

    @pl.loop(0, doms)
    def _(s):
        if small:
            count_seeds((doms - 1 + s) * share, (doms + s) * share)
        q = lax.rem(me - s + doms, doms)
        plane(q, 0, (everything, beside), side).wait_recv()
        plane(q, 5, (everything, beside), mate).start()
        plane(q, 1, (everything, across), over).wait_recv()
        plane(q, 3, (everything, across), side).start()
        plane(q, 6, (everything, across), mate).start()

    if small:
        count_seeds(early, total_seeds)

    @pl.loop(0, doms)
    def _(s):
        q = lax.rem(me - s + doms, doms)
        plane(q, 3, (everything, corner), side).wait_recv()
        plane(q, 7, (everything, corner), mate).start()

    local_two.wait()

    @pl.loop(0, doms)
    def _(s):
        q = lax.rem(me - s + doms, doms)
        for k in range(4):
            plane(q, 4 + k, (everything, theirs[k]), mate).wait_recv()

    @pl.loop(0, doms // group)
    def _(part):
        block = full[pl.ds(part * group, group)].reshape(step_rows, full.shape[2])
        start = pl.multiple_of(part * step_rows, step_rows)
        there = pl.ds(pl.multiple_of(w * known + start, step_rows), step_rows)
        rows[there, :] = product(block, w_second[w]).astype(BF16)

    two_copy.wait_recv()

    @pl.loop(0, doms // group)
    def _(part):
        block = full[pl.ds(part * group, group)].reshape(step_rows, full.shape[2])
        start = pl.multiple_of(part * step_rows, step_rows)
        there = pl.ds(pl.multiple_of((1 - w) * known + start, step_rows), step_rows)
        rows[there, :] = product(block, w_second[1 - w]).astype(BF16)

    chunk = 512 if small else second_c.shape[1]

    @pl.loop(0, total_seeds, step=chunk)
    def _(start):
        start = pl.multiple_of(start, chunk)
        if small:
            counted = second_c[:, pl.ds(start, chunk)]
        else:
            count_seeds(start, start + chunk, start)
            counted = second_c[...]
        share_of_one = seed_count[pl.ds(start, chunk), :1]
        out[pl.ds(start, chunk), :] = (turned_product(counted, rows[...]) * share_of_one).astype(BF16)

    one_copy.wait_send()
    two_copy.wait_send()

    @pl.loop(1, doms)
    def _(s):
        p = lax.rem(me + s, doms)
        fetch_copy(s, me, p).wait_send()
        hidden_copy(s, me, p).wait_send()

    @pl.loop(0, doms)
    def _(q):
        pass_copy(q, core).wait_send()
        plane(q, 0, (everything, mine), side).wait_send()
        plane(q, 1, (everything, mine), over).wait_send()
        plane(q, 3, (everything, across), side).wait_send()
        plane(q, 4, (everything, mine), mate).wait_send()
        plane(q, 5, (everything, beside), mate).wait_send()
        plane(q, 6, (everything, across), mate).wait_send()
        plane(q, 7, (everything, corner), mate).wait_send()


def shards(
    doms,
    store_feat,
    want_in,
    nbr_in,
    self_in,
    count_in,
    weight_one,
    want_hid,
    nbr_hid,
    self_hid,
    count_hid,
    weight_two,
):
    stored, features = store_feat.shape
    r0, r1 = want_in.shape[2], want_hid.shape[2]
    t1, fan_one = nbr_in.shape
    t2, fan_two = nbr_hid.shape
    width = weight_one.shape[1] // 2
    columns = weight_two.shape[1]
    group = math.gcd(doms, 4)
    known = doms * r1
    counted = t2 if doms == group else 256

    def padded(fan):
        return fan + 2 + -(fan + 2) % 8

    vmem = pl.BlockSpec(memory_space=pltpu.VMEM)
    smem = pl.BlockSpec(memory_space=pltpu.SMEM)
    dma = pltpu.SemaphoreType.DMA
    return pl.pallas_call(
        functools.partial(kernel, (doms, fan_one, fan_two)),
        out_shape=jax.ShapeDtypeStruct((t2, columns), BF16),
        in_specs=[smem, smem] + [vmem] * 9,
        out_specs=vmem,
        scratch_shapes=[
            pltpu.VMEM((stored, features), F32),
            pltpu.VMEM((t1, padded(fan_one)), F32),
            pltpu.VMEM((doms * r1, padded(fan_one)), F32),
            pltpu.VMEM((doms, r0 // 2, features), BF16),
            pltpu.VMEM((doms, 2, r0 // 2, features), BF16),
            pltpu.VMEM((2, features, width), BF16),
            pltpu.VMEM((2,) + weight_two.shape, BF16),
            pltpu.VMEM((doms, r1, width), BF16),
            pltpu.VMEM((2 * doms * r0, group * r1), BF16),
            pltpu.VMEM((doms, r1, weight_two.shape[0]), BF16),
            pltpu.VMEM((2 * known, columns), BF16),
            pltpu.VMEM((padded(fan_two), t2), F32),
            pltpu.VMEM((t2, 8), F32),
            pltpu.VMEM((2 * known, counted), BF16),
            dma((2,)), dma((2,)), dma((2,)),
            dma((doms,)), dma((doms,)), dma((doms,)), dma((doms,)), dma((doms,)), dma((doms,)),
            dma((doms, 8)), dma((doms, 8)),
        ],
        compiler_params=pltpu.CompilerParams(
            collective_id=0, has_side_effects=True, vmem_limit_bytes=56 << 20
        ),
    )(
        want_in[0], want_hid[0], store_feat, nbr_in.T, self_in[None], count_in[None], weight_one,
        nbr_hid.T, self_hid[None], count_hid[None], weight_two,
    )


def solution(mesh):
    return jax.shard_map(
        functools.partial(shards, mesh.shape["dom"]),
        mesh=mesh,
        in_specs=(
            P("dom", None),
            P("dom", None, None),
            P("dom", None),
            P("dom"),
            P("dom"),
            P("wt", "hid"),
            P("dom", None, None),
            P("dom", None),
            P("dom"),
            P("dom"),
            P("wt", "hid"),
        ),
        out_specs=P("dom", "hid"),
        check_vma=False,
    )
```
